256 devices in a mesh: wide: 16 (over y, x_hi, core), blk: 16 (over x_lo, z).
Axes of the slice: x: 4 (x_hi: 2, x_lo: 2; x = x_hi * 2 + x_lo), y: 4, z: 8, core: 2. Of those that a mesh axis runs over, the one named last changes fastest.
Arguments:
- lam: bfloat16 [512, 768, 768], P('blk', 'wide'), may hold values from -6 to 6
- ints: bfloat16 [768, 768, 2, 768], P('wide', 'blk'), may hold values from -0.0078125 to 0.0078125
Outputs:
- ladder: float32 [512, 2, 768], P(('wide', 'blk'))
The draws below stay inside these ranges and needn't reach their ends.
All inputs are finite; a program needn't handle non-finite values.
Results may differ from the reference program's by a relative error of at most 0.0003.
Values may be sent and summed in bfloat16 or wider, within the bound.
No kernel may reach another device: no remote copies, remote signals or barrier semaphores. Data moves between devices by JAX's collectives and lax.ppermute only.
A program may use at most 128 MiB of HBM per device.

```python
import jax
import jax.numpy as jnp
from jax import lax

NV = 768
A_SLAB = 2
IJ = 512


def strengthened(values, stream_key, source, target, blocks, factor):
    owner, partner = [(jnp.arange(values.shape[axis_at]) // (values.shape[axis_at] // blocks)).reshape([-1 if axis == axis_at else 1 for axis in range(values.ndim)]) for axis_at in (source, target)]
    chosen = jax.random.permutation(stream_key, blocks)[partner]
    strong = (owner == chosen) | (owner == (partner + blocks // 2) % blocks)
    return jnp.where(strong, factor * values, values)


def block_scale(stream_key, dims, cuts, least, high):
    def one(dim, parts):
        steps = jax.random.uniform(jax.random.fold_in(jax.random.fold_in(stream_key, 6), dim), (parts,), jnp.float32, least / len(cuts), high / len(cuts))
        return jnp.repeat(jnp.exp(steps), dims[dim] // parts).reshape((-1,) + (1,) * (len(dims) - dim - 1))

    loudness = one(*cuts[0])
    for cut in cuts[1:]:
        loudness = loudness * one(*cut)
    return loudness


def normal_values(rng, shape, deviation, limit, cuts=(), kind=jnp.bfloat16):
    array = jax.random.normal(rng, shape, jnp.float32) * deviation
    if len(cuts) > 0:
        array = block_scale(rng, shape, cuts, -0.22, 0.18) * array
    return jnp.clip(array, min=-limit, max=limit).astype(kind)


def gaussian_with(rng, dims, width, bound, cuts, heavy, kind=jnp.bfloat16):
    drawn = width * jax.random.normal(rng, dims, jnp.float32)
    if cuts:
        drawn = drawn * block_scale(rng, dims, cuts, -0.22, 0.18)
    return jnp.clip(strengthened(drawn, jax.random.fold_in(rng, 3), *heavy), -bound, bound).astype(kind)


def setup_inputs(seed: int = 0) -> dict:
    key_of = jax.random.split(jax.random.key(seed), 3)
    return {
        "lam": gaussian_with(key_of[0], (IJ, NV, NV), 1.0, 6.0, ((0, 16), (1, 16)), (1, 0, 16, 2.0)),
        "ints": normal_values(key_of[1], (NV, NV, A_SLAB, NV), (NV * NV) ** -0.5, 0.0078125, ((0, 16), (1, 16))),
    }


def reference(lam, ints):
    block = NV // 16
    lam_blocks = lam.reshape(IJ, 16, block, NV).transpose(1, 0, 2, 3)
    int_blocks = ints.reshape(16, block * NV, A_SLAB * NV)

    def step(total, pieces):
        left, right = pieces
        product = jnp.dot(left.reshape(IJ, block * NV), right, preferred_element_type=jnp.float32)
        return total + product, None

    start = jnp.zeros((IJ, A_SLAB * NV), jnp.float32)
    total, _ = lax.scan(step, start, (lam_blocks, int_blocks))
    return (0.5 * total).reshape(IJ, A_SLAB, NV)
```

```python
import jax
import jax.numpy as jnp
from jax import lax
from jax.experimental import pallas as pl
from jax.experimental.pallas import tpu as pltpu
from jax.sharding import Mesh, PartitionSpec as P

AXES = ("y", "xh", "core", "xl", "z")
SIZES = (4, 2, 2, 2, 8)
MIB = 1024 * 1024


def pack_kernel(lam_ref, out_ref, pick_ref):
    @pl.when(pl.program_id(0) == 0)
    def _():
        rows = lax.broadcasted_iota(jnp.int32, (512, 512), 0)
        cols = lax.broadcasted_iota(jnp.int32, (512, 512), 1)
        wanted = (2 * (rows % 16) + (rows // 16) % 2) * 16 + rows // 32
        pick_ref[...] = jnp.where(cols == wanted, 1.0, 0.0).astype(jnp.bfloat16)

    x = lam_ref[...].reshape(512, 768)
    y = jnp.dot(pick_ref[...], x, preferred_element_type=jnp.float32).astype(jnp.bfloat16)
    y = y.reshape(16, 2, 16, 768)
    for core in range(2):
        for j in range(16):
            out_ref[core * 16 + j] = jnp.concatenate(
                [y[c, core, :, 48 * j : 48 * j + 48] for c in range(16)], axis=-1
            )


def pack(lam):
    return pl.pallas_call(
        pack_kernel,
        grid=(3,),
        in_specs=[pl.BlockSpec((32, 16, 768), lambda m: (0, m, 0))],
        out_specs=pl.BlockSpec((32, 16, 768), lambda m: (0, 0, m)),
        out_shape=jax.ShapeDtypeStruct((32, 16, 2304), jnp.bfloat16),
        scratch_shapes=[pltpu.VMEM((512, 512), jnp.bfloat16)],
        compiler_params=pltpu.CompilerParams(vmem_limit_bytes=60 * MIB),
        cost_estimate=pl.CostEstimate(flops=3 * 2 * 512 * 512 * 768, bytes_accessed=4 * 1179648, transcendentals=0),
        name="pack",
    )(lam)


def product_kernel(core_ref, x_ref, w_own_ref, w_oth_ref, out_ref, held, acc_ref, sems):
    depth, steps = 384, 6
    copies = []
    for s, w in enumerate((w_own_ref, w_oth_ref)):
        for k in range(steps):
            copies.append(pltpu.make_async_copy(w.at[pl.ds(k * depth, depth)], held.at[s, k], sems.at[s, k]))
            copies[-1].start()
    core = core_ref[0]
    for s in range(2):
        x = x_ref.at[core if s == 0 else 1 - core]
        for k in range(steps):
            copies[s * steps + k].wait()
            lhs = x[:, :, k * depth : (k + 1) * depth].reshape(256, depth)
            for n in range(0, 1536, 512):
                term = jnp.dot(lhs, held[s, k, :, n : n + 512], preferred_element_type=jnp.float32)
                if s + k == 0:
                    acc_ref[:, n : n + 512] = term
                elif s * steps + k < 2 * steps - 1:
                    acc_ref[:, n : n + 512] += term
                else:
                    acc = (0.5 * (acc_ref[:, n : n + 512] + term)).reshape(8, 2, 2, 8, 512)
                    for c in range(2):
                        for x1 in range(2):
                            out_ref[:, x1, c, :, n : n + 512] = acc[:, c, x1]


def product(core, received, w_own, w_oth):
    return pl.pallas_call(
        product_kernel,
        in_specs=[
            pl.BlockSpec(memory_space=pltpu.SMEM),
            pl.BlockSpec(memory_space=pltpu.VMEM),
            pl.BlockSpec(memory_space=pl.ANY),
            pl.BlockSpec(memory_space=pl.ANY),
        ],
        out_specs=pl.BlockSpec(memory_space=pltpu.VMEM),
        out_shape=jax.ShapeDtypeStruct((8, 2, 2, 8, 1536), jnp.float32),
        scratch_shapes=[
            pltpu.VMEM((2, 6, 384, 1536), jnp.bfloat16),
            pltpu.VMEM((256, 1536), jnp.float32),
            pltpu.SemaphoreType.DMA((2, 6)),
        ],
        compiler_params=pltpu.CompilerParams(vmem_limit_bytes=20 * MIB),
        cost_estimate=pl.CostEstimate(flops=2 * 256 * 4608 * 1536, bytes_accessed=18 * MIB, transcendentals=0),
        name="product",
    )(core, received.reshape(2, 16, 16, 2304), *[pltpu.with_memory_space_constraint(w, pltpu.HBM) for w in (w_own, w_oth)])


def shards(lam, ints):
    core = lax.axis_index("core").astype(jnp.int32).reshape(1)
    ints_oth = lax.ppermute(ints, "core", [(0, 1), (1, 0)])
    w_own, w_oth = ints.reshape(2304, 1536), ints_oth.reshape(2304, 1536)
    received = lax.all_to_all(pack(lam), ("core", "xl", "z"), 0, 0)
    part = product(core, received, w_own, w_oth).reshape(16, 16, 1536)
    part = lax.all_to_all(part, ("y", "xh", "xl"), 0, 0).sum(0)
    part = lax.all_to_all(part.reshape(16, 12, 128), ("core", "z"), 0, 0)
    return part.reshape(2, 8, 12, 128).sum(1).reshape(2, 2, 768)


def solution(mesh):
    fine = Mesh(mesh.devices.reshape(SIZES), AXES)
    wide, blk = AXES[:3], AXES[3:]
    in_specs = (P(blk, wide, None), P(wide, blk, None, None))
    out_specs = P(AXES, None, None)
    return jax.shard_map(shards, mesh=fine, in_specs=in_specs, out_specs=out_specs, check_vma=False)
```

```python
import itertools

import jax
import jax.numpy as jnp
from jax import lax
from jax.experimental import pallas as pl
from jax.experimental.pallas import tpu as pltpu
from jax.sharding import Mesh, PartitionSpec as P

AXES = ("y", "xh", "core", "xl", "z")
SIZES = (4, 2, 2, 2, 8)
MIB = 1024 * 1024


def pack_kernel(lam_ref, out_ref, pick_ref):
    @pl.when(pl.program_id(0) == 0)
    def _():
        rows = lax.broadcasted_iota(jnp.int32, (512, 512), 0)
        cols = lax.broadcasted_iota(jnp.int32, (512, 512), 1)
        wanted = (2 * (rows % 16) + (rows // 16) % 2) * 16 + rows // 32
        pick_ref[...] = jnp.where(cols == wanted, 1.0, 0.0).astype(jnp.bfloat16)

    x = lam_ref[...].reshape(512, 768)
    y = jnp.dot(pick_ref[...], x, preferred_element_type=jnp.float32).astype(jnp.bfloat16)
    y = y.reshape(16, 2, 16, 768)
    for core in range(2):
        for j in range(16):
            out_ref[core * 16 + j] = jnp.concatenate(
                [y[c, core, :, 48 * j : 48 * j + 48] for c in range(16)], axis=-1
            )


def pack(lam):
    return pl.pallas_call(
        pack_kernel,
        grid=(3,),
        in_specs=[pl.BlockSpec((32, 16, 768), lambda m: (0, m, 0))],
        out_specs=pl.BlockSpec((32, 16, 768), lambda m: (0, 0, m)),
        out_shape=jax.ShapeDtypeStruct((32, 16, 2304), jnp.bfloat16),
        scratch_shapes=[pltpu.VMEM((512, 512), jnp.bfloat16)],
        compiler_params=pltpu.CompilerParams(vmem_limit_bytes=60 * MIB),
        cost_estimate=pl.CostEstimate(flops=3 * 2 * 512 * 512 * 768, bytes_accessed=4 * 1179648, transcendentals=0),
        name="pack",
    )(lam)


DEPTH = 256
STEPS = 2304 // DEPTH


def product_kernel(at_ref, x_ref, w_own_ref, w_oth_ref, *rest):
    outs, (held, acc_ref, sems) = rest[:4], rest[4:]
    copies = []
    for s, w in enumerate((w_own_ref, w_oth_ref)):
        for k in range(STEPS):
            copies.append(pltpu.make_async_copy(w.at[pl.ds(k * DEPTH, DEPTH)], held.at[s, k], sems.at[s, k]))
            copies[-1].start()
    core, me = at_ref[0], at_ref[1]
    for s in range(2):
        x = x_ref.at[core if s == 0 else 1 - core]
        for k in range(STEPS):
            copies[s * STEPS + k].wait()
            lhs = x[:, :, k * DEPTH : (k + 1) * DEPTH].reshape(256, DEPTH)
            for n in range(0, 1536, 512):
                term = jnp.dot(lhs, held[s, k, :, n : n + 512], preferred_element_type=jnp.float32)
                if s + k == 0:
                    acc_ref[:, n : n + 512] = term
                else:
                    acc_ref[:, n : n + 512] += term
    for flip, out_ref in enumerate(outs):
        for j in range(4):
            gone = me ^ flip
            y = jnp.where(core == 0, gone, j)
            x = jnp.where(core == 0, j, gone)
            for c in range(2):
                row = (((y * 2 + x // 2) * 2 + c) * 2 + x % 2) * 8
                out_ref[j, 8 * c : 8 * c + 8] = 0.5 * acc_ref[pl.ds(pl.multiple_of(row, 8), 8), :]


def product(at, received, w_own, w_oth):
    in_hbm = [pltpu.with_memory_space_constraint(w, pltpu.HBM) for w in (w_own, w_oth)]
    return pl.pallas_call(
        product_kernel,
        in_specs=[
            pl.BlockSpec(memory_space=pltpu.SMEM),
            pl.BlockSpec(memory_space=pltpu.VMEM),
            pl.BlockSpec(memory_space=pl.ANY),
            pl.BlockSpec(memory_space=pl.ANY),
        ],
        out_specs=[pl.BlockSpec(memory_space=pltpu.VMEM)] * 4,
        out_shape=[jax.ShapeDtypeStruct((4, 16, 1536), jnp.float32)] * 4,
        scratch_shapes=[
            pltpu.VMEM((2, STEPS, DEPTH, 1536), jnp.bfloat16),
            pltpu.VMEM((256, 1536), jnp.float32),
            pltpu.SemaphoreType.DMA((2, STEPS)),
        ],
        compiler_params=pltpu.CompilerParams(vmem_limit_bytes=20 * MIB),
        cost_estimate=pl.CostEstimate(flops=2 * 256 * 4608 * 1536, bytes_accessed=18 * MIB, transcendentals=0),
        name="product",
    )(at, received.reshape(2, 16, 16, 2304), *in_hbm)


def pairs(flip, first):
    out = []
    for y, x, core in itertools.product(range(4), range(4), range(2)):
        to_y, to_x = (y ^ flip, x) if core == first else (y, x ^ flip)
        out.append(tuple(((b * 2 + a // 2) * 2 + core) * 2 + a % 2 for b, a in ((y, x), (to_y, to_x))))
    return out


def moved(piece, flip, first):
    return lax.ppermute(piece, ("y", "xh", "core", "xl"), pairs(flip, first))


def shards(lam, ints):
    core = lax.axis_index("core").astype(jnp.int32)
    y, x = lax.axis_index("y").astype(jnp.int32), lax.axis_index(("xh", "xl")).astype(jnp.int32)
    early, late = jnp.where(core == 0, y, x), jnp.where(core == 0, x, y)
    ints_oth = lax.ppermute(ints, "core", [(0, 1), (1, 0)])
    w_own, w_oth = ints.reshape(2304, 1536), ints_oth.reshape(2304, 1536)
    received = lax.all_to_all(pack(lam), ("core", "xl", "z"), 0, 0)
    part = product(jnp.stack([core, early]), received, w_own, w_oth)
    total = part[0]
    for flip in (2, 1, 3):
        total = total + moved(part[flip], flip, 0)
    pieces = [lax.dynamic_index_in_dim(total, late ^ flip, 0, keepdims=False) for flip in range(4)]
    total = pieces[0]
    for flip in (2, 1, 3):
        total = total + moved(pieces[flip], flip, 1)
    total = lax.all_to_all(total.reshape(16, 12, 128), ("core", "z"), 0, 0)
    return total.reshape(2, 8, 12, 128).sum(1).reshape(2, 2, 768)


def solution(mesh):
    fine = Mesh(mesh.devices.reshape(SIZES), AXES)
    wide, blk = AXES[:3], AXES[3:]
    in_specs = (P(blk, wide, None), P(wide, blk, None, None))
    out_specs = P(AXES, None, None)
    return jax.shard_map(shards, mesh=fine, in_specs=in_specs, out_specs=out_specs, check_vma=False)
```

```python
import itertools

import jax
import jax.numpy as jnp
from jax import lax
from jax.experimental import pallas as pl
from jax.experimental.pallas import tpu as pltpu
from jax.sharding import Mesh, PartitionSpec as P

AXES = ("y", "xh", "core", "xl", "z")
SIZES = (4, 2, 2, 2, 8)
MIB = 1024 * 1024


def pack_kernel(lam_ref, out_ref, taken, made, pick_ref, in_sems, out_sems):
    ins = [pltpu.make_async_copy(lam_ref.at[:, pl.ds(16 * m, 16)], taken.at[m], in_sems.at[m]) for m in range(3)]
    for copy in ins:
        copy.start()
    rows = lax.broadcasted_iota(jnp.int32, (512, 512), 0)
    cols = lax.broadcasted_iota(jnp.int32, (512, 512), 1)
    wanted = (2 * (rows % 16) + (rows // 16) % 2) * 16 + rows // 32
    pick_ref[...] = jnp.where(cols == wanted, 1.0, 0.0).astype(jnp.bfloat16)
    outs = []
    for m in range(3):
        ins[m].wait()
        y = jnp.dot(pick_ref[...], taken[m].reshape(512, 768), preferred_element_type=jnp.float32)
        y = y.astype(jnp.bfloat16).reshape(16, 2, 16, 768)
        for core in range(2):
            for j in range(16):
                made[m, core * 16 + j] = jnp.concatenate(
                    [y[c, core, :, 48 * j : 48 * j + 48] for c in range(16)], axis=-1
                )
        outs.append(pltpu.make_async_copy(made.at[m], out_ref.at[:, :, pl.ds(768 * m, 768)], out_sems.at[m]))
        outs[m].start()
    for copy in outs:
        copy.wait()


def pack(lam):
    return pl.pallas_call(
        pack_kernel,
        in_specs=[pl.BlockSpec(memory_space=pl.ANY)],
        out_specs=pl.BlockSpec(memory_space=pl.ANY),
        out_shape=jax.ShapeDtypeStruct((32, 16, 2304), jnp.bfloat16),
        scratch_shapes=[
            pltpu.VMEM((3, 32, 16, 768), jnp.bfloat16),
            pltpu.VMEM((3, 32, 16, 768), jnp.bfloat16),
            pltpu.VMEM((512, 512), jnp.bfloat16),
            pltpu.SemaphoreType.DMA((3,)),
            pltpu.SemaphoreType.DMA((3,)),
        ],
        compiler_params=pltpu.CompilerParams(vmem_limit_bytes=60 * MIB),
        cost_estimate=pl.CostEstimate(flops=3 * 2 * 512 * 512 * 768, bytes_accessed=4 * 1179648, transcendentals=0),
        name="pack",
    )(lam)


DEPTH = 256
STEPS = 2304 // DEPTH


def product_kernel(at_ref, x_ref, w_own_ref, w_oth_ref, *rest):
    outs, (held, acc_ref, sems) = rest[:4], rest[4:]
    copies = []
    for s, w in enumerate((w_own_ref, w_oth_ref)):
        for k in range(STEPS):
            copies.append(pltpu.make_async_copy(w.at[pl.ds(k * DEPTH, DEPTH)], held.at[s, k], sems.at[s, k]))
            copies[-1].start()
    core, y, x_at = at_ref[0], at_ref[1], at_ref[2]
    blocks = [(y ^ (p // 4)) * 4 + ((x_at // 2) ^ (p // 2 % 2)) * 2 + p % 2 for p in range(16)]
    swap = x_at % 2 == 1

    def term(s, k, n):
        x = x_ref.at[core if s == 0 else 1 - core]
        lhs = jnp.concatenate([x[block, :, k * DEPTH : (k + 1) * DEPTH] for block in blocks], axis=0)
        return jnp.dot(lhs, held[s, k, :, n : n + 512], preferred_element_type=jnp.float32)

    for s in range(2):
        for k in range(STEPS):
            copies[s * STEPS + k].wait()
            if (s, k) == (1, STEPS - 1):
                break
            for n in range(0, 1536, 512):
                if s + k == 0:
                    acc_ref[:, n : n + 512] = term(s, k, n)
                else:
                    acc_ref[:, n : n + 512] += term(s, k, n)

    def total(n):
        return (0.5 * (acc_ref[:, n : n + 512] + term(1, STEPS - 1, n))).reshape(16, 2, 8, 512)

    for first in range(2):

        @pl.when(core == first)
        def _():
            for n in range(0, 1536, 512):
                done = total(n)
                for (flip, out_ref), late, c in itertools.product(enumerate(outs), range(4), range(2)):
                    flip_y, flip_x = (flip, late) if first == 0 else (late, flip)
                    rows = done[(flip_y * 2 + flip_x // 2) * 2 + c]
                    low, high = rows[flip_x % 2], rows[1 - flip_x % 2]
                    out_ref[late, 8 * c : 8 * c + 8, n : n + 512] = jnp.where(swap, high, low)


def product(at, received, w_own, w_oth):
    in_hbm = [pltpu.with_memory_space_constraint(w, pltpu.HBM) for w in (w_own, w_oth)]
    return pl.pallas_call(
        product_kernel,
        in_specs=[
            pl.BlockSpec(memory_space=pltpu.SMEM),
            pl.BlockSpec(memory_space=pltpu.VMEM),
            pl.BlockSpec(memory_space=pl.ANY),
            pl.BlockSpec(memory_space=pl.ANY),
        ],
        out_specs=[pl.BlockSpec(memory_space=pltpu.VMEM)] * 4,
        out_shape=[pltpu.VMEM((4, 16, 1536), jnp.float32)] * 4,
        scratch_shapes=[
            pltpu.VMEM((2, STEPS, DEPTH, 1536), jnp.bfloat16),
            pltpu.VMEM((256, 1536), jnp.float32),
            pltpu.SemaphoreType.DMA((2, STEPS)),
        ],
        compiler_params=pltpu.CompilerParams(vmem_limit_bytes=20 * MIB),
        cost_estimate=pl.CostEstimate(flops=2 * 256 * 4608 * 1536, bytes_accessed=18 * MIB, transcendentals=0),
        name="product",
    )(at, received.reshape(2, 16, 16, 2304), *in_hbm)


def pairs(flip, first):
    out = []
    for y, x, core in itertools.product(range(4), range(4), range(2)):
        to_y, to_x = (y ^ flip, x) if core == first else (y, x ^ flip)
        out.append(tuple(((b * 2 + a // 2) * 2 + core) * 2 + a % 2 for b, a in ((y, x), (to_y, to_x))))
    return out


def moved(piece, flip, first):
    return lax.ppermute(piece, ("y", "xh", "core", "xl"), pairs(flip, first))


def shards(lam, ints):
    core = lax.axis_index("core").astype(jnp.int32)
    y, x = lax.axis_index("y").astype(jnp.int32), lax.axis_index(("xh", "xl")).astype(jnp.int32)
    ints_oth = lax.ppermute(ints, "core", [(0, 1), (1, 0)])
    w_own, w_oth = ints.reshape(2304, 1536), ints_oth.reshape(2304, 1536)
    received = lax.all_to_all(pack(lam), ("core", "xl", "z"), 0, 0)
    part = product(jnp.stack([core, y, x]), received, w_own, w_oth)
    total = part[0]
    for flip in (2, 1, 3):
        total = total + moved(part[flip], flip, 0)
    pieces = [total[flip] for flip in range(4)]
    total = pieces[0]
    for flip in (2, 1, 3):
        total = total + moved(pieces[flip], flip, 1)
    total = lax.all_to_all(total.reshape(16, 12, 128), ("core", "z"), 0, 0)
    return total.reshape(2, 8, 12, 128).sum(1).reshape(2, 2, 768)


def solution(mesh):
    fine = Mesh(mesh.devices.reshape(SIZES), AXES)
    wide, blk = AXES[:3], AXES[3:]
    in_specs = (P(blk, wide, None), P(wide, blk, None, None))
    out_specs = P(AXES, None, None)
    return jax.shard_map(shards, mesh=fine, in_specs=in_specs, out_specs=out_specs, check_vma=False)
```

```python
import itertools

import jax
import jax.numpy as jnp
from jax import lax
from jax.experimental import pallas as pl
from jax.experimental.pallas import tpu as pltpu
from jax.sharding import Mesh, PartitionSpec as P

AXES = ("y", "xh", "core", "xl", "z")
SIZES = (4, 2, 2, 2, 8)
MIB = 1024 * 1024


def pack_kernel(lam_ref, out_ref, taken, made, pick_ref, in_sems, out_sems):
    ins = [pltpu.make_async_copy(lam_ref.at[:, pl.ds(16 * m, 16)], taken.at[m], in_sems.at[m]) for m in range(3)]
    for copy in ins:
        copy.start()
    rows = lax.broadcasted_iota(jnp.int32, (256, 256), 0)
    cols = lax.broadcasted_iota(jnp.int32, (256, 256), 1)
    wanted = (2 * (rows % 8) + (rows // 8) % 2) * 16 + rows // 16
    pick_ref[...] = jnp.where(cols == wanted, 1.0, 0.0).astype(jnp.bfloat16)
    outs = []
    for m in range(3):
        ins[m].wait()
        halves = [
            jnp.dot(pick_ref[...], taken[m, 16 * h : 16 * h + 16].reshape(256, 768), preferred_element_type=jnp.float32)
            for h in range(2)
        ]
        halves = [half.reshape(16, 2, 8, 768) for half in halves]
        for core in range(2):
            y = jnp.concatenate([half[:, core] for half in halves], axis=1).astype(jnp.bfloat16)
            for j in range(16):
                made[m, core * 16 + j] = jnp.concatenate(
                    [y[c, :, 48 * j : 48 * j + 48] for c in range(16)], axis=-1
                )
        outs.append(pltpu.make_async_copy(made.at[m], out_ref.at[:, :, pl.ds(768 * m, 768)], out_sems.at[m]))
        outs[m].start()
    for copy in outs:
        copy.wait()


def pack(lam):
    return pl.pallas_call(
        pack_kernel,
        in_specs=[pl.BlockSpec(memory_space=pl.ANY)],
        out_specs=pl.BlockSpec(memory_space=pl.ANY),
        out_shape=jax.ShapeDtypeStruct((32, 16, 2304), jnp.bfloat16),
        scratch_shapes=[
            pltpu.VMEM((3, 32, 16, 768), jnp.bfloat16),
            pltpu.VMEM((3, 32, 16, 768), jnp.bfloat16),
            pltpu.VMEM((256, 256), jnp.bfloat16),
            pltpu.SemaphoreType.DMA((3,)),
            pltpu.SemaphoreType.DMA((3,)),
        ],
        compiler_params=pltpu.CompilerParams(vmem_limit_bytes=60 * MIB),
        cost_estimate=pl.CostEstimate(flops=3 * 4 * 256 * 256 * 768, bytes_accessed=4 * 1179648, transcendentals=0),
        name="pack",
    )(lam)


DEPTH = 256
STEPS = 2304 // DEPTH


def product_kernel(at_ref, x_ref, w_own_ref, w_oth_ref, *rest):
    outs, (held, acc_ref, sems) = rest[:4], rest[4:]
    copies = []
    for s, w in enumerate((w_own_ref, w_oth_ref)):
        for k in range(STEPS):
            copies.append(pltpu.make_async_copy(w.at[pl.ds(k * DEPTH, DEPTH)], held.at[s, k], sems.at[s, k]))
            copies[-1].start()
    core, y, x_at = at_ref[0], at_ref[1], at_ref[2]
    blocks = [(y ^ (p // 4)) * 4 + ((x_at // 2) ^ (p // 2 % 2)) * 2 + p % 2 for p in range(16)]
    swap = x_at % 2 == 1

    def term(s, k, n):
        x = x_ref.at[core if s == 0 else 1 - core]
        lhs = jnp.concatenate([x[block, :, k * DEPTH : (k + 1) * DEPTH] for block in blocks], axis=0)
        return jnp.dot(lhs, held[s, k, :, n : n + 512], preferred_element_type=jnp.float32)

    for s in range(2):
        for k in range(STEPS):
            copies[s * STEPS + k].wait()
            if (s, k) == (1, STEPS - 1):
                break
            for n in range(0, 1536, 512):
                if s + k == 0:
                    acc_ref[:, n : n + 512] = term(s, k, n)
                else:
                    acc_ref[:, n : n + 512] += term(s, k, n)

    def total(n):
        return (0.5 * (acc_ref[:, n : n + 512] + term(1, STEPS - 1, n))).reshape(16, 2, 8, 512)

    for first in range(2):

        @pl.when(core == first)
        def _():
            for n in range(0, 1536, 512):
                done = total(n)
                for (flip, out_ref), late, c in itertools.product(enumerate(outs), range(4), range(2)):
                    flip_y, flip_x = (flip, late) if first == 0 else (late, flip)
                    rows = done[(flip_y * 2 + flip_x // 2) * 2 + c]
                    low, high = rows[flip_x % 2], rows[1 - flip_x % 2]
                    out_ref[late, 8 * c : 8 * c + 8, n : n + 512] = jnp.where(swap, high, low)


def product(at, received, w_own, w_oth):
    in_hbm = [pltpu.with_memory_space_constraint(w, pltpu.HBM) for w in (w_own, w_oth)]
    return pl.pallas_call(
        product_kernel,
        in_specs=[
            pl.BlockSpec(memory_space=pltpu.SMEM),
            pl.BlockSpec(memory_space=pltpu.VMEM),
            pl.BlockSpec(memory_space=pl.ANY),
            pl.BlockSpec(memory_space=pl.ANY),
        ],
        out_specs=[pl.BlockSpec(memory_space=pltpu.VMEM)] * 4,
        out_shape=[pltpu.VMEM((4, 16, 1536), jnp.float32)] * 4,
        scratch_shapes=[
            pltpu.VMEM((2, STEPS, DEPTH, 1536), jnp.bfloat16),
            pltpu.VMEM((256, 1536), jnp.float32),
            pltpu.SemaphoreType.DMA((2, STEPS)),
        ],
        compiler_params=pltpu.CompilerParams(vmem_limit_bytes=20 * MIB),
        cost_estimate=pl.CostEstimate(flops=2 * 256 * 4608 * 1536, bytes_accessed=18 * MIB, transcendentals=0),
        name="product",
    )(at, received.reshape(2, 16, 16, 2304), *in_hbm)


def pairs(flip, first):
    out = []
    for y, x, core in itertools.product(range(4), range(4), range(2)):
        to_y, to_x = (y ^ flip, x) if core == first else (y, x ^ flip)
        out.append(tuple(((b * 2 + a // 2) * 2 + core) * 2 + a % 2 for b, a in ((y, x), (to_y, to_x))))
    return out


def moved(piece, flip, first):
    return lax.ppermute(piece, ("y", "xh", "core", "xl"), pairs(flip, first))


def shards(lam, ints):
    core = lax.axis_index("core").astype(jnp.int32)
    y, x = lax.axis_index("y").astype(jnp.int32), lax.axis_index(("xh", "xl")).astype(jnp.int32)
    ints, sent = lax.optimization_barrier((ints, pack(lam)))
    ints_oth = lax.ppermute(ints, "core", [(0, 1), (1, 0)])
    w_own, w_oth = ints.reshape(2304, 1536), ints_oth.reshape(2304, 1536)
    received = lax.all_to_all(sent, ("core", "xl", "z"), 0, 0)
    part = product(jnp.stack([core, y, x]), received, w_own, w_oth)
    total = part[0]
    for flip in (2, 1, 3):
        total = total + moved(part[flip], flip, 0)
    pieces = [total[flip] for flip in range(4)]
    total = pieces[0]
    for flip in (2, 1, 3):
        total = total + moved(pieces[flip], flip, 1)
    total = lax.all_to_all(total.reshape(16, 2, 768), ("core", "z"), 0, 0)
    return total.reshape(2, 8, 2, 768).sum(1)


def solution(mesh):
    fine = Mesh(mesh.devices.reshape(SIZES), AXES)
    wide, blk = AXES[:3], AXES[3:]
    in_specs = (P(blk, wide, None), P(wide, blk, None, None))
    out_specs = P(AXES, None, None)
    return jax.shard_map(shards, mesh=fine, in_specs=in_specs, out_specs=out_specs, check_vma=False)
```

```python
import itertools

import jax
import jax.numpy as jnp
from jax import lax
from jax.experimental import pallas as pl
from jax.experimental.pallas import tpu as pltpu
from jax.sharding import Mesh, PartitionSpec as P

AXES = ("y", "xh", "core", "xl", "z")
SIZES = (4, 2, 2, 2, 8)
MIB = 1024 * 1024


def pack_kernel(lam_ref, out_ref, taken, made, pick_ref, in_sems, out_sems):
    ins = [pltpu.make_async_copy(lam_ref.at[:, pl.ds(16 * m, 16)], taken.at[m], in_sems.at[m]) for m in range(3)]
    for copy in ins:
        copy.start()
    rows = lax.broadcasted_iota(jnp.int32, (256, 256), 0)
    cols = lax.broadcasted_iota(jnp.int32, (256, 256), 1)
    wanted = (2 * (rows % 8) + (rows // 8) % 2) * 16 + rows // 16
    pick_ref[...] = jnp.where(cols == wanted, 1.0, 0.0).astype(jnp.bfloat16)
    outs = []
    for m in range(3):
        ins[m].wait()
        halves = [
            jnp.dot(pick_ref[...], taken[m, 16 * h : 16 * h + 16].reshape(256, 768), preferred_element_type=jnp.float32)
            for h in range(2)
        ]
        halves = [half.reshape(16, 2, 8, 768) for half in halves]
        for core in range(2):
            y = jnp.concatenate([half[:, core] for half in halves], axis=1).astype(jnp.bfloat16)
            for j in range(16):
                made[m, core * 16 + j] = jnp.concatenate(
                    [y[c, :, 48 * j : 48 * j + 48] for c in range(16)], axis=-1
                )
        outs.append(pltpu.make_async_copy(made.at[m], out_ref.at[:, :, pl.ds(768 * m, 768)], out_sems.at[m]))
        outs[m].start()
    for copy in outs:
        copy.wait()


def pack(lam):
    return pl.pallas_call(
        pack_kernel,
        in_specs=[pl.BlockSpec(memory_space=pl.ANY)],
        out_specs=pl.BlockSpec(memory_space=pl.ANY),
        out_shape=jax.ShapeDtypeStruct((32, 16, 2304), jnp.bfloat16),
        scratch_shapes=[
            pltpu.VMEM((3, 32, 16, 768), jnp.bfloat16),
            pltpu.VMEM((3, 32, 16, 768), jnp.bfloat16),
            pltpu.VMEM((256, 256), jnp.bfloat16),
            pltpu.SemaphoreType.DMA((3,)),
            pltpu.SemaphoreType.DMA((3,)),
        ],
        compiler_params=pltpu.CompilerParams(vmem_limit_bytes=60 * MIB),
        cost_estimate=pl.CostEstimate(flops=3 * 4 * 256 * 256 * 768, bytes_accessed=4 * 1179648, transcendentals=0),
        name="pack",
    )(lam)


RUNS = [(s, row, min(512, 2304 - row)) for s in range(2) for row in range(0, 2304, 512)]


def product_kernel(at_ref, x_ref, w_own_ref, w_oth_ref, *rest):
    outs, (held, acc_ref, sems) = rest[:4], rest[4:]
    copies = []
    for i, (s, row, depth) in enumerate(RUNS):
        at = pl.ds(row, depth)
        copies.append(pltpu.make_async_copy((w_own_ref, w_oth_ref)[s].at[at], held.at[s, at], sems.at[i]))
        copies[-1].start()
    core, y, x_at = at_ref[0], at_ref[1], at_ref[2]
    blocks = [(y ^ (p // 4)) * 4 + ((x_at // 2) ^ (p // 2 % 2)) * 2 + p % 2 for p in range(16)]
    swap = x_at % 2 == 1

    def term(run, n):
        s, row, depth = run
        x = x_ref.at[core if s == 0 else 1 - core]
        lhs = jnp.concatenate([x[block, :, row : row + depth] for block in blocks], axis=0)
        return jnp.dot(lhs, held[s, row : row + depth, n : n + 512], preferred_element_type=jnp.float32)

    for i, run in enumerate(RUNS[:-1]):
        copies[i].wait()
        for n in range(0, 1536, 512):
            if i == 0:
                acc_ref[:, n : n + 512] = term(run, n)
            else:
                acc_ref[:, n : n + 512] += term(run, n)
    copies[-1].wait()

    def total(n):
        return (0.5 * (acc_ref[:, n : n + 512] + term(RUNS[-1], n))).reshape(16, 2, 8, 512)

    for first in range(2):

        @pl.when(core == first)
        def _():
            for n in range(0, 1536, 512):
                done = total(n)
                for (flip, out_ref), late, c in itertools.product(enumerate(outs), range(4), range(2)):
                    flip_y, flip_x = (flip, late) if first == 0 else (late, flip)
                    rows = done[(flip_y * 2 + flip_x // 2) * 2 + c]
                    low, high = rows[flip_x % 2], rows[1 - flip_x % 2]
                    out_ref[late, 8 * c : 8 * c + 8, n : n + 512] = jnp.where(swap, high, low)


def product(at, received, w_own, w_oth):
    in_hbm = [pltpu.with_memory_space_constraint(w, pltpu.HBM) for w in (w_own, w_oth)]
    return pl.pallas_call(
        product_kernel,
        in_specs=[
            pl.BlockSpec(memory_space=pltpu.SMEM),
            pl.BlockSpec(memory_space=pltpu.VMEM),
            pl.BlockSpec(memory_space=pl.ANY),
            pl.BlockSpec(memory_space=pl.ANY),
        ],
        out_specs=[pl.BlockSpec(memory_space=pltpu.VMEM)] * 4,
        out_shape=[pltpu.VMEM((4, 16, 1536), jnp.float32)] * 4,
        scratch_shapes=[
            pltpu.VMEM((2, 2304, 1536), jnp.bfloat16),
            pltpu.VMEM((256, 1536), jnp.float32),
            pltpu.SemaphoreType.DMA((len(RUNS),)),
        ],
        compiler_params=pltpu.CompilerParams(vmem_limit_bytes=20 * MIB),
        cost_estimate=pl.CostEstimate(flops=2 * 256 * 4608 * 1536, bytes_accessed=18 * MIB, transcendentals=0),
        name="product",
    )(at, received.reshape(2, 16, 16, 2304), *in_hbm)


def pairs(flip, first):
    out = []
    for y, x, core in itertools.product(range(4), range(4), range(2)):
        to_y, to_x = (y ^ flip, x) if core == first else (y, x ^ flip)
        out.append(tuple(((b * 2 + a // 2) * 2 + core) * 2 + a % 2 for b, a in ((y, x), (to_y, to_x))))
    return out


def moved(piece, flip, first):
    return lax.ppermute(piece, ("y", "xh", "core", "xl"), pairs(flip, first))


def shards(lam, ints):
    core = lax.axis_index("core").astype(jnp.int32)
    y, x = lax.axis_index("y").astype(jnp.int32), lax.axis_index(("xh", "xl")).astype(jnp.int32)
    ints, sent = lax.optimization_barrier((ints, pack(lam)))
    ints_oth = lax.ppermute(ints, "core", [(0, 1), (1, 0)])
    w_own, w_oth = ints.reshape(2304, 1536), ints_oth.reshape(2304, 1536)
    received = lax.all_to_all(sent, ("core", "xl", "z"), 0, 0)
    part = product(jnp.stack([core, y, x]), received, w_own, w_oth)
    total = part[0]
    for flip in (2, 1, 3):
        total = total + moved(part[flip], flip, 0)
    pieces = [total[flip] for flip in range(4)]
    total = pieces[0]
    for flip in (2, 1, 3):
        total = total + moved(pieces[flip], flip, 1)
    total = lax.all_to_all(total.reshape(16, 2, 768), ("core", "z"), 0, 0)
    return total.reshape(2, 8, 2, 768).sum(1)


def solution(mesh):
    fine = Mesh(mesh.devices.reshape(SIZES), AXES)
    wide, blk = AXES[:3], AXES[3:]
    in_specs = (P(blk, wide, None), P(wide, blk, None, None))
    out_specs = P(AXES, None, None)
    return jax.shard_map(shards, mesh=fine, in_specs=in_specs, out_specs=out_specs, check_vma=False)
```
